128 devices in a mesh: row: 16 (over z, x), col: 8 (over y, core).
Axes of the slice: x: 4, y: 4, z: 4, core: 2. Of those that a mesh axis runs over, the one named last changes fastest.
Arguments:
- integrals: float32 [12800, 3200], P('row', 'col'), may hold values from -0.109375 to 0.109375
- amplitudes: float32 [8, 40, 400, 400], P('col', None, 'row'), may hold values from -6 to 6
Outputs:
- residual: float32 [12800, 16000], P('row', 'col')
The draws below stay inside these ranges and needn't reach their ends.
All inputs are finite; a program needn't handle non-finite values.
Results may differ from the reference program's by a relative error of at most 0.00007.
Values sent between devices are 32-bit elements; how exact they have to be, the bound alone decides.
No kernel may reach another device: no remote copies, remote signals or barrier semaphores. Data moves between devices by JAX's collectives and lax.ppermute only.
A program may use at most 192 MiB of HBM per device.

```python
import jax
import jax.numpy as jnp
from jax import lax

O = 40
V = 400
K_OCC = 8
I_OCC = 32


def block_scale(own_key, dims, split, smallest, top_value):
    def one(dim, parts):
        steps = jax.random.uniform(jax.random.fold_in(jax.random.fold_in(own_key, 6), dim), (parts,), jnp.float32, smallest / len(split), top_value / len(split))
        return jnp.repeat(jnp.exp(steps), dims[dim] // parts).reshape((-1,) + (1,) * (len(dims) - dim - 1))

    level = one(*split[0])
    for cut in split[1:]:
        level = level * one(*cut)
    return level


def noise(rng, dims, scale, bound, shards=(), dtype=jnp.bfloat16):
    drawn = jax.random.normal(rng, dims, jnp.float32) * scale
    if len(shards) > 0:
        drawn = block_scale(rng, dims, shards, -0.22, 0.18) * drawn
    return jnp.clip(drawn, min=-bound, max=bound).astype(dtype)


def setup_inputs(seed: int = 0) -> dict:
    key_list = jax.random.split(jax.random.key(seed), 3)
    integrals = noise(key_list[0], (I_OCC * V, V * K_OCC), (V * K_OCC) ** -0.5, 0.109375, ((0, 16), (1, 8)), jnp.float32)
    amplitudes = noise(key_list[1], (K_OCC, O, V, V), 1.0, 6.0, ((0, 8), (2, 16)), jnp.float32)
    return dict(integrals=integrals, amplitudes=amplitudes)


def reference(integrals, amplitudes):
    amp_ph = jnp.transpose(amplitudes, (3, 0, 1, 2)).reshape(V * K_OCC, O * V)
    return jnp.dot(integrals, amp_ph, precision=lax.Precision.HIGHEST, preferred_element_type=jnp.float32)
```

```python
import functools

import jax
import jax.numpy as jnp
from jax import lax
from jax.experimental import pallas as pl
from jax.experimental.pallas import tpu as pltpu
from jax.sharding import PartitionSpec as P

Z, X, Y, CORES = 4, 4, 4, 2
AXES = ("row", "col")
LANES = 128


def permutation(move):
    pairs = []
    for z in range(Z):
        for x in range(X):
            for y in range(Y):
                for core in range(CORES):
                    to_z, to_x, to_y, to_core = move(z, x, y, core)
                    source = ((z * X + x) * Y + y) * CORES + core
                    target = (((to_z % Z) * X + to_x % X) * Y + to_y % Y) * CORES + to_core
                    pairs.append((source, target))
    return pairs


def send_y(value, distance):
    return lax.ppermute(value, AXES, permutation(lambda z, x, y, core: (z, x, y + distance, core)))


def send_core(value):
    return lax.ppermute(value, AXES, permutation(lambda z, x, y, core: (z, x, y, 1 - core)))


def send_first(value, distance):
    return lax.ppermute(
        value,
        AXES,
        permutation(lambda z, x, y, core: (z + distance * core, x + distance * (1 - core), y, core)),
    )


def send_second(value, distance):
    return lax.ppermute(
        value,
        AXES,
        permutation(lambda z, x, y, core: (z + distance * (1 - core), x + distance * core, y, core)),
    )


def regrid_kernel(j_block, place_ref, amp_ref, out_ref, rows):
    b_here, occupied, virtual = amp_ref.shape
    rows[...] = jnp.zeros_like(rows)
    for q in range(occupied // j_block):
        for j in range(j_block):
            rows[j * b_here : (j + 1) * b_here, :virtual] = amp_ref[:, q * j_block + j, :]
        out_ref[place_ref[q]] = rows[...].T[:virtual]


def regrid(amp, places, j_block):
    b_here, occupied, virtual = amp.shape
    blocks = occupied // j_block
    padded = pl.cdiv(virtual, LANES) * LANES
    return pl.pallas_call(
        functools.partial(regrid_kernel, j_block),
        out_shape=jax.ShapeDtypeStruct((blocks, virtual, LANES), jnp.float32),
        in_specs=[
            pl.BlockSpec(memory_space=pltpu.SMEM),
            pl.BlockSpec(memory_space=pltpu.VMEM),
        ],
        out_specs=pl.BlockSpec(memory_space=pltpu.VMEM),
        scratch_shapes=[pltpu.VMEM((LANES, padded), jnp.float32)],
        compiler_params=pltpu.CompilerParams(vmem_limit_bytes=32 * 2**20),
        name="regrid",
    )(places, amp)


def split(value):
    high = value.astype(jnp.bfloat16)
    low = (value - high.astype(jnp.float32)).astype(jnp.bfloat16)
    return high, low


def panel_kernel(k_total, slot_ref, panel_ref, high_ref, low_ref, ordered):
    depth = panel_ref.shape[0]
    virtual = depth // k_total
    for k in range(k_total):
        start = pl.multiple_of(slot_ref[k] * virtual, 8)
        ordered[pl.ds(start, virtual), :] = panel_ref[pl.ds(k, virtual, stride=k_total), :]
    high_ref[...], low_ref[...] = split(ordered[...].T)


def panels_by_k(panel, slots, k_total):
    depth, rows = panel.shape
    return pl.pallas_call(
        functools.partial(panel_kernel, k_total),
        out_shape=[jax.ShapeDtypeStruct((rows, depth), jnp.bfloat16)] * 2,
        grid=(pl.cdiv(rows, LANES),),
        in_specs=[
            pl.BlockSpec(memory_space=pltpu.SMEM),
            pl.BlockSpec((depth, LANES), lambda i: (0, i)),
        ],
        out_specs=[pl.BlockSpec((LANES, depth), lambda i: (i, 0))] * 2,
        scratch_shapes=[pltpu.VMEM((depth, LANES), jnp.float32)],
        compiler_params=pltpu.CompilerParams(vmem_limit_bytes=32 * 2**20),
        name="panels",
    )(slots, panel)


def product_kernel(pieces, *refs):
    high_ref, low_ref = refs[:2]
    piece_refs = refs[2 : 2 + pieces]
    out_ref, total = refs[2 + pieces :]
    step = pl.program_id(0)

    @pl.when(step == 0)
    def _():
        total[...] = jnp.zeros_like(total)

    high, low = split(jnp.concatenate([ref[...] for ref in piece_refs], axis=1))
    dot = functools.partial(jnp.dot, preferred_element_type=jnp.float32)
    total[...] += dot(high_ref[...], high) + (dot(high_ref[...], low) + dot(low_ref[...], high))

    @pl.when(step == pl.num_programs(0) - 1)
    def _():
        for i in range(pieces):
            out_ref[i] = total[:, i * LANES : (i + 1) * LANES]


def product(high, low, pieces, depth_block=640):
    rows, depth = high.shape
    n = len(pieces)
    return pl.pallas_call(
        functools.partial(product_kernel, n),
        out_shape=jax.ShapeDtypeStruct((n, rows, LANES), jnp.float32),
        grid=(depth // depth_block,),
        in_specs=[pl.BlockSpec((rows, depth_block), lambda i: (0, i))] * 2
        + [pl.BlockSpec((depth_block, LANES), lambda i: (i, 0))] * n,
        out_specs=pl.BlockSpec((n, rows, LANES), lambda i: (0, 0, 0)),
        scratch_shapes=[pltpu.VMEM((rows, n * LANES), jnp.float32)],
        compiler_params=pltpu.CompilerParams(vmem_limit_bytes=40 * 2**20),
        cost_estimate=pl.CostEstimate(
            flops=6 * rows * depth * n * LANES,
            bytes_accessed=4 * depth * (rows + n * LANES),
            transcendentals=0,
        ),
        name="product",
    )(high, low, *pieces)


def order_kernel(j_block, b_here, places_ref, *refs):
    *group_refs, out_ref, by_row = refs
    slot = 0
    for ref in group_refs:
        for i in range(ref.shape[0]):
            by_row[places_ref[slot]] = ref[i]
            slot += 1
    rows, width = out_ref.shape
    blocks = by_row.shape[0]
    virtual = blocks * b_here
    lane = lax.broadcasted_iota(jnp.int32, (rows, LANES), 1)
    for tile in range(pl.cdiv(width, LANES)):
        first = tile * LANES
        last = min(first + LANES, width)
        value = jnp.zeros((rows, LANES), jnp.float32)
        for j in range(j_block):
            for block in range(blocks):
                start = j * virtual + block * b_here
                if start >= last or start + b_here <= first:
                    continue
                moved = pltpu.roll(by_row[block], (start - first - j * b_here) % LANES, 1)
                inside = (lane >= start - first) & (lane < start - first + b_here)
                value = jnp.where(inside, moved, value)
        out_ref[:, first:last] = value[:, : last - first]


def order(groups, places, j_block, b_here, row_block=80):
    blocks = sum(group.shape[0] for group in groups)
    rows = groups[0].shape[1]
    width = blocks * b_here * j_block
    return pl.pallas_call(
        functools.partial(order_kernel, j_block, b_here),
        out_shape=jax.ShapeDtypeStruct((rows, width), jnp.float32),
        grid=(rows // row_block,),
        in_specs=[pl.BlockSpec(memory_space=pltpu.SMEM)]
        + [pl.BlockSpec((g.shape[0], row_block, LANES), lambda i: (0, i, 0)) for g in groups],
        out_specs=pl.BlockSpec((row_block, width), lambda i: (i, 0)),
        scratch_shapes=[pltpu.VMEM((blocks, row_block, LANES), jnp.float32)],
        compiler_params=pltpu.CompilerParams(vmem_limit_bytes=32 * 2**20),
        name="order",
    )(places, *groups)


def per_device(integrals, amplitudes):
    rows_here = lax.axis_size("row")
    cols_here = lax.axis_size("col")
    k_here, occupied, b_here, virtual = amplitudes.shape
    j_block = occupied // cols_here
    k_total = k_here * cols_here
    row, col = lax.axis_index("row"), lax.axis_index("col")
    z, x, y, core = row // X, row % X, col // CORES, col % CORES

    panel = lax.all_gather(integrals.T, "col", axis=0, tiled=True)

    q = jnp.arange(cols_here, dtype=jnp.int32)
    away = (q // CORES - y) % Y
    other = (q % CORES) ^ core
    kept = regrid(amplitudes[0].transpose(1, 0, 2), other * Y + away, j_block)
    kept, given = kept[:Y], kept[Y:]
    pairs = jnp.concatenate([kept, send_core(given)], axis=1)
    own = jnp.concatenate(
        [pairs[0], send_y(pairs[1], 1), send_y(pairs[3], -1), send_y(pairs[2], 2)], axis=0
    )

    before = send_first(own, 1)
    after = send_first(own, -1)
    half = own.shape[0] // 2
    across = jnp.concatenate([send_first(before[:half], 1), send_first(after[half:], -1)], axis=0)
    line = [own, before, after, across]
    line_offset = [0, -1, 1, 2]
    second_before = [send_second(piece, 1) for piece in line]
    second_after = [send_second(piece, -1) for piece in line]
    second_across = [
        send_second(second_before[i], 1) if i % 2 == 0 else send_second(second_after[i], -1)
        for i in range(4)
    ]

    slot_of_away = jnp.array([0, 1, 3, 2], jnp.int32)
    k = jnp.arange(k_total, dtype=jnp.int32)
    slots = 2 * slot_of_away[(y - k // CORES) % Y] + ((k % CORES) ^ core)
    high, low = panels_by_k(panel, slots, k_total)

    grouped = [
        [(line[i], line_offset[i], 0) for i in range(4)],
        [(s[i], line_offset[i], d) for i in (0, 1) for s, d in ((second_before, -1), (second_after, 1))],
        [(s[i], line_offset[i], d) for i in (2, 3) for s, d in ((second_before, -1), (second_after, 1))],
        [(second_across[i], line_offset[i], 2) for i in range(4)],
    ]
    products, places = [], []
    for group in grouped:
        products.append(product(high, low, [piece for piece, _, _ in group]))
        for _, first, second in group:
            from_core0 = ((z + second) % Z) * X + (x + first) % X
            from_core1 = ((z + first) % Z) * X + (x + second) % X
            places.append(jnp.where(core == 0, from_core0, from_core1))
    return order(products, jnp.stack(places).astype(jnp.int32), j_block, b_here)


def solution(mesh):
    return jax.shard_map(
        per_device,
        mesh=mesh,
        in_specs=(P("row", "col"), P("col", None, "row", None)),
        out_specs=P("row", "col"),
        check_vma=False,
    )
```

```python
import functools

import jax
import jax.numpy as jnp
from jax import lax
from jax.experimental import pallas as pl
from jax.experimental.pallas import tpu as pltpu
from jax.sharding import PartitionSpec as P

Z, X, Y, CORES = 4, 4, 4, 2
AXES = ("row", "col")
LANES = 128


def permutation(move):
    pairs = []
    for z in range(Z):
        for x in range(X):
            for y in range(Y):
                for core in range(CORES):
                    to_z, to_x, to_y, to_core = move(z, x, y, core)
                    source = ((z * X + x) * Y + y) * CORES + core
                    target = (((to_z % Z) * X + to_x % X) * Y + to_y % Y) * CORES + to_core
                    pairs.append((source, target))
    return pairs


def send_y(value, distance):
    return lax.ppermute(value, AXES, permutation(lambda z, x, y, core: (z, x, y + distance, core)))


def send_core(value):
    return lax.ppermute(value, AXES, permutation(lambda z, x, y, core: (z, x, y, 1 - core)))


def send_first(value, distance):
    return lax.ppermute(
        value,
        AXES,
        permutation(lambda z, x, y, core: (z + distance * core, x + distance * (1 - core), y, core)),
    )


def send_second(value, distance):
    return lax.ppermute(
        value,
        AXES,
        permutation(lambda z, x, y, core: (z + distance * (1 - core), x + distance * core, y, core)),
    )


def rotation(block, b_here, virtual, j_block):
    middle = j_block // 2
    return (middle * (virtual - b_here) + block * b_here) % LANES


def regrid_kernel(j_block, place_ref, amp_ref, out_ref, rows):
    b_here, occupied, virtual = amp_ref.shape
    rows[...] = jnp.zeros_like(rows)
    for q in range(occupied // j_block):
        for j in range(j_block):
            rows[j * b_here : (j + 1) * b_here, :virtual] = amp_ref[:, q * j_block + j, :]
        out_ref[place_ref[q]] = pltpu.roll(rows[...].T[:virtual], place_ref[occupied // j_block], 1)


def regrid(amp, places, j_block):
    b_here, occupied, virtual = amp.shape
    blocks = occupied // j_block
    padded = pl.cdiv(virtual, LANES) * LANES
    return pl.pallas_call(
        functools.partial(regrid_kernel, j_block),
        out_shape=jax.ShapeDtypeStruct((blocks, virtual, LANES), jnp.float32),
        in_specs=[
            pl.BlockSpec(memory_space=pltpu.SMEM),
            pl.BlockSpec(memory_space=pltpu.VMEM),
        ],
        out_specs=pl.BlockSpec(memory_space=pltpu.VMEM),
        scratch_shapes=[pltpu.VMEM((LANES, padded), jnp.float32)],
        compiler_params=pltpu.CompilerParams(vmem_limit_bytes=32 * 2**20),
        name="regrid",
    )(places, amp)


def split(value):
    high = value.astype(jnp.bfloat16)
    low = (value - high.astype(jnp.float32)).astype(jnp.bfloat16)
    return high, low


def panel_kernel(k_total, slot_ref, panel_ref, high_ref, low_ref, ordered):
    depth = panel_ref.shape[0]
    virtual = depth // k_total
    for k in range(k_total):
        start = pl.multiple_of(slot_ref[k] * virtual, 8)
        ordered[pl.ds(start, virtual), :] = panel_ref[pl.ds(k, virtual, stride=k_total), :]
    high_ref[...], low_ref[...] = split(ordered[...].T)


def panels_by_k(panel, slots, k_total):
    depth, rows = panel.shape
    return pl.pallas_call(
        functools.partial(panel_kernel, k_total),
        out_shape=[jax.ShapeDtypeStruct((rows, depth), jnp.bfloat16)] * 2,
        grid=(pl.cdiv(rows, LANES),),
        in_specs=[
            pl.BlockSpec(memory_space=pltpu.SMEM),
            pl.BlockSpec((depth, LANES), lambda i: (0, i)),
        ],
        out_specs=[pl.BlockSpec((LANES, depth), lambda i: (i, 0))] * 2,
        scratch_shapes=[pltpu.VMEM((depth, LANES), jnp.float32)],
        compiler_params=pltpu.CompilerParams(vmem_limit_bytes=32 * 2**20),
        name="panels",
    )(slots, panel)


def fill(pieces, high_ref, low_ref):
    for i, parts in enumerate(pieces):
        start = 0
        for ref in parts:
            rows = slice(start, start + ref.shape[0])
            lanes = slice(i * LANES, (i + 1) * LANES)
            high_ref[rows, lanes], low_ref[rows, lanes] = split(ref[...])
            start += ref.shape[0]


def three_products(panel_high, panel_low, high, low):
    dot = functools.partial(jnp.dot, preferred_element_type=jnp.float32)
    return dot(panel_high, high) + (dot(panel_high, low) + dot(panel_low, high))


def product_kernel(chunks, *refs):
    panel_high, panel_low, *piece_refs, out_ref, high, low = refs
    pieces = [piece_refs[i : i + chunks] for i in range(0, len(piece_refs), chunks)]
    for i in range(0, len(pieces), 2):
        fill(pieces[i : i + 2], high, low)
        value = three_products(panel_high[...], panel_low[...], high[...], low[...])
        out_ref[i] = value[:, :LANES]
        out_ref[i + 1] = value[:, LANES:]


def product(panel_high, panel_low, pieces):
    rows, depth = panel_high.shape
    n = len(pieces)
    return pl.pallas_call(
        functools.partial(product_kernel, len(pieces[0])),
        out_shape=jax.ShapeDtypeStruct((n, rows, LANES), jnp.float32),
        in_specs=[pl.BlockSpec(memory_space=pltpu.VMEM)] * (2 + n * len(pieces[0])),
        out_specs=pl.BlockSpec(memory_space=pltpu.VMEM),
        scratch_shapes=[pltpu.VMEM((depth, 2 * LANES), jnp.bfloat16)] * 2,
        compiler_params=pltpu.CompilerParams(vmem_limit_bytes=12 * 2**20),
        cost_estimate=pl.CostEstimate(
            flops=6 * rows * depth * n * LANES,
            bytes_accessed=4 * depth * (rows + n * LANES),
            transcendentals=0,
        ),
        name="product",
    )(panel_high, panel_low, *[part for piece in pieces for part in piece])


def order_kernel(j_block, b_here, places_ref, *refs):
    *group_refs, out_ref, by_row = refs
    blocks = by_row.shape[0]
    slot = 0
    for ref in group_refs:
        for i in range(ref.shape[0]):
            by_row[places_ref[slot]] = ref[i].reshape(by_row.shape[1:])
            slot += 1
    for missing in range(slot, blocks):
        by_row[places_ref[missing]] = jnp.zeros(by_row.shape[1:], jnp.float32)
    rows, width = out_ref.shape
    virtual = blocks * b_here
    middle = j_block // 2
    lane = lax.broadcasted_iota(jnp.int32, (8, LANES), 1)
    moved = {}
    for tile in range(pl.cdiv(width, LANES)):
        first = tile * LANES
        last = min(first + LANES, width)
        value = None
        for j in range(j_block):
            turn = (j - middle) * (virtual - b_here) % LANES
            for block in range(blocks):
                start = j * virtual + block * b_here
                if start >= last or start + b_here <= first:
                    continue
                if (j, block) not in moved:
                    moved[j, block] = pltpu.roll(by_row[block], turn, 2) if turn else by_row[block]
                piece = moved[j, block]
                value = piece if value is None else jnp.where((lane >= start - first)[None], piece, value)
        out_ref[:, first:last] = value.reshape(rows, LANES)[:, : last - first]


def order(groups, places, j_block, b_here, row_block=80):
    blocks = places.shape[0]
    rows = groups[0].shape[1]
    width = blocks * b_here * j_block
    return pl.pallas_call(
        functools.partial(order_kernel, j_block, b_here),
        out_shape=jax.ShapeDtypeStruct((rows, width), jnp.float32),
        grid=(rows // row_block,),
        in_specs=[pl.BlockSpec(memory_space=pltpu.SMEM)]
        + [pl.BlockSpec((g.shape[0], row_block, LANES), lambda i: (0, i, 0)) for g in groups],
        out_specs=pl.BlockSpec((row_block, width), lambda i: (i, 0)),
        scratch_shapes=[pltpu.VMEM((blocks, row_block // 8, 8, LANES), jnp.float32)],
        compiler_params=pltpu.CompilerParams(vmem_limit_bytes=16 * 2**20),
        name="order",
    )(places, *groups)


def last_kernel(chunks, *refs):
    panel_high, panel_low, place_ref, *piece_refs, done_ref, out_ref, high, low = refs
    step = pl.program_id(0)

    @pl.when(step == 0)
    def _():
        fill([piece_refs[:chunks], piece_refs[chunks:]], high, low)

    rows = out_ref.shape[0]
    here = pl.ds(pl.multiple_of(step * rows, 16), rows)
    value = three_products(panel_high[here, :], panel_low[here, :], high[...], low[...])
    dot = functools.partial(jnp.dot, preferred_element_type=jnp.float32)
    first, second = split(value)
    out_ref[...] = done_ref[here, :] + (dot(first, place_ref[...]) + dot(second, place_ref[...]))


def last_product(panel_high, panel_low, pieces, place, done, row_block=400):
    rows, depth = panel_high.shape
    width = done.shape[1]
    whole = pl.BlockSpec(memory_space=pltpu.VMEM)
    return pl.pallas_call(
        functools.partial(last_kernel, len(pieces[0])),
        out_shape=jax.ShapeDtypeStruct((rows, width), jnp.float32),
        grid=(rows // row_block,),
        in_specs=[whole] * (4 + 2 * len(pieces[0])),
        out_specs=pl.BlockSpec((row_block, width), lambda i: (i, 0)),
        scratch_shapes=[pltpu.VMEM((depth, 2 * LANES), jnp.bfloat16)] * 2,
        compiler_params=pltpu.CompilerParams(vmem_limit_bytes=20 * 2**20),
        name="last",
    )(panel_high, panel_low, place, *[part for piece in pieces for part in piece], done)


def after(value, *others):
    return lax.optimization_barrier((value, *others))[0]


def per_device(integrals, amplitudes):
    rows_here = lax.axis_size("row")
    cols_here = lax.axis_size("col")
    k_here, occupied, b_here, virtual = amplitudes.shape
    j_block = occupied // cols_here
    k_total = k_here * cols_here
    row, col = lax.axis_index("row"), lax.axis_index("col")
    z, x, y, core = row // X, row % X, col // CORES, col % CORES

    q = jnp.arange(cols_here, dtype=jnp.int32)
    away = (q // CORES - y) % Y
    other = (q % CORES) ^ core
    virtual_blocks = rows_here * b_here
    turn = rotation(row, b_here, virtual_blocks, j_block)
    places = jnp.append(other * Y + away, turn).astype(jnp.int32)
    kept = regrid(amplitudes[0].transpose(1, 0, 2), places, j_block)
    kept, given = kept[:Y], kept[Y:]
    pairs = jnp.concatenate([kept, send_core(given)], axis=1)
    own = jnp.concatenate(
        [pairs[0], send_y(pairs[1], 1), send_y(pairs[3], -1), send_y(pairs[2], 2)], axis=0
    )
    panel = lax.all_gather(after(integrals.T, own), "col", axis=0, tiled=True)

    before, behind = send_first(own, 1), send_first(own, -1)
    half = own.shape[0] // 2
    across = jnp.concatenate([send_first(before[:half], 1), send_first(behind[half:], -1)], axis=0)
    line = [own, before, behind, across]
    line_offset = [0, -1, 1, 2]
    second_before = [send_second(piece, 1) for piece in line]
    second_after = [send_second(piece, -1) for piece in line]

    slot_of_away = jnp.array([0, 1, 3, 2], jnp.int32)
    k = jnp.arange(k_total, dtype=jnp.int32)
    slots = 2 * slot_of_away[(y - k // CORES) % Y] + ((k % CORES) ^ core)
    high, low = panels_by_k(after(panel, second_before[1], second_after[1]), slots, k_total)

    def place(i, second):
        first = line_offset[i]
        from_core0 = ((z + second) % Z) * X + (x + first) % X
        from_core1 = ((z + first) % Z) * X + (x + second) % X
        return jnp.where(core == 0, from_core0, from_core1)

    def both_sides(lines):
        return [(side[i],) for i in lines for side in (second_before, second_after)]

    first_line = (after(own, second_before[2], second_after[2]),)
    products = [product(high, low, [first_line] + [(piece,) for piece in line[1:]])]
    places = [place(i, 0) for i in range(4)]
    second_across = [send_second(second_before[0], 1), send_second(second_after[1], -1)]
    products.append(product(after(high, products[0]), low, both_sides((0, 1))))
    places += [place(i, second) for i in (0, 1) for second in (-1, 1)]
    second_across += [
        send_second(after(second_before[2], products[1]), 1),
        send_second(after(second_after[3], products[1]), -1),
    ]
    products.append(product(after(high, products[1]), low, both_sides((2, 3))))
    places += [place(i, second) for i in (2, 3) for second in (-1, 1)]
    products.append(product(after(high, products[2]), low, [(piece,) for piece in second_across[:2]]))
    places += [place(i, 2) for i in range(4)]
    places = jnp.stack(places).astype(jnp.int32)
    done = order(products, places, j_block, b_here)

    position = (jnp.arange(LANES, dtype=jnp.int32) - rotation(places[-2:, None], b_here, virtual_blocks, j_block)) % LANES
    column = (position // b_here) * virtual_blocks + places[-2:, None] * b_here + position % b_here
    column = jnp.where(position < j_block * b_here, column, -1).reshape(-1, 1)
    one_hot = (column == jnp.arange(done.shape[1], dtype=jnp.int32)).astype(jnp.bfloat16)
    return last_product(high, low, [(piece,) for piece in second_across[2:]], one_hot, done)


def solution(mesh):
    return jax.shard_map(
        per_device,
        mesh=mesh,
        in_specs=(P("row", "col"), P("col", None, "row", None)),
        out_specs=P("row", "col"),
        check_vma=False,
    )
```

```python
import functools

import jax
import jax.numpy as jnp
from jax import lax
from jax.experimental import pallas as pl
from jax.experimental.pallas import tpu as pltpu
from jax.sharding import PartitionSpec as P

Z, X, Y, CORES = 4, 4, 4, 2
AXES = ("row", "col")
LANES = 128


def permutation(move):
    pairs = []
    for z in range(Z):
        for x in range(X):
            for y in range(Y):
                for core in range(CORES):
                    to_z, to_x, to_y, to_core = move(z, x, y, core)
                    source = ((z * X + x) * Y + y) * CORES + core
                    target = (((to_z % Z) * X + to_x % X) * Y + to_y % Y) * CORES + to_core
                    pairs.append((source, target))
    return pairs


def send_y(value, distance):
    return lax.ppermute(value, AXES, permutation(lambda z, x, y, core: (z, x, y + distance, core)))


def send_core(value):
    return lax.ppermute(value, AXES, permutation(lambda z, x, y, core: (z, x, y, 1 - core)))


def send_first(value, distance):
    return lax.ppermute(
        value,
        AXES,
        permutation(lambda z, x, y, core: (z + distance * core, x + distance * (1 - core), y, core)),
    )


def send_second(value, distance):
    return lax.ppermute(
        value,
        AXES,
        permutation(lambda z, x, y, core: (z + distance * (1 - core), x + distance * core, y, core)),
    )


def rotation(block, b_here, virtual, j_block):
    middle = j_block // 2
    return (middle * (virtual - b_here) + block * b_here) % LANES


def regrid_kernel(j_block, place_ref, amp_ref, out_ref, rows):
    b_here, occupied, virtual = amp_ref.shape
    rows[...] = jnp.zeros_like(rows)
    for q in range(occupied // j_block):
        for j in range(j_block):
            rows[j * b_here : (j + 1) * b_here, :virtual] = amp_ref[:, q * j_block + j, :]
        out_ref[place_ref[q]] = pltpu.roll(rows[...].T[:virtual], place_ref[occupied // j_block], 1)


def regrid(amp, places, j_block):
    b_here, occupied, virtual = amp.shape
    blocks = occupied // j_block
    padded = pl.cdiv(virtual, LANES) * LANES
    return pl.pallas_call(
        functools.partial(regrid_kernel, j_block),
        out_shape=jax.ShapeDtypeStruct((blocks, virtual, LANES), jnp.float32),
        in_specs=[
            pl.BlockSpec(memory_space=pltpu.SMEM),
            pl.BlockSpec(memory_space=pltpu.VMEM),
        ],
        out_specs=pl.BlockSpec(memory_space=pltpu.VMEM),
        scratch_shapes=[pltpu.VMEM((LANES, padded), jnp.float32)],
        compiler_params=pltpu.CompilerParams(vmem_limit_bytes=8 * 2**20),
        name="regrid",
    )(places, amp)


def split(value):
    high = value.astype(jnp.bfloat16)
    low = (value - high.astype(jnp.float32)).astype(jnp.bfloat16)
    return high, low


def panel_kernel(k_total, slot_ref, panel_ref, high_ref, low_ref, ordered):
    depth = panel_ref.shape[0]
    virtual = depth // k_total
    for k in range(k_total):
        start = pl.multiple_of(slot_ref[k] * virtual, 8)
        ordered[pl.ds(start, virtual), :] = panel_ref[pl.ds(k, virtual, stride=k_total), :]
    high_ref[...], low_ref[...] = split(ordered[...].T)


def panels_by_k(panel, slots, k_total):
    depth, rows = panel.shape
    return pl.pallas_call(
        functools.partial(panel_kernel, k_total),
        out_shape=[jax.ShapeDtypeStruct((rows, depth), jnp.bfloat16)] * 2,
        grid=(pl.cdiv(rows, LANES),),
        in_specs=[
            pl.BlockSpec(memory_space=pltpu.SMEM),
            pl.BlockSpec((depth, LANES), lambda i: (0, i)),
        ],
        out_specs=[pl.BlockSpec((LANES, depth), lambda i: (i, 0))] * 2,
        scratch_shapes=[pltpu.VMEM((depth, LANES), jnp.float32)],
        compiler_params=pltpu.CompilerParams(vmem_limit_bytes=14 * 2**20),
        name="panels",
    )(slots, panel)


def fill(pieces, high_ref, low_ref):
    for i, parts in enumerate(pieces):
        start = 0
        for ref in parts:
            rows = slice(start, start + ref.shape[0])
            lanes = slice(i * LANES, (i + 1) * LANES)
            high_ref[rows, lanes], low_ref[rows, lanes] = split(ref[...])
            start += ref.shape[0]


def three_products(panel_high, panel_low, high, low):
    dot = functools.partial(jnp.dot, preferred_element_type=jnp.float32)
    return dot(panel_high, high) + (dot(panel_high, low) + dot(panel_low, high))


def product_kernel(chunks, *refs):
    panel_high, panel_low, *piece_refs, out_ref, high, low = refs
    pieces = [piece_refs[i : i + chunks] for i in range(0, len(piece_refs), chunks)]
    for i in range(0, len(pieces), 2):
        fill(pieces[i : i + 2], high, low)
        value = three_products(panel_high[...], panel_low[...], high[...], low[...])
        out_ref[i] = value[:, :LANES]
        out_ref[i + 1] = value[:, LANES:]


def product(panel_high, panel_low, pieces):
    rows, depth = panel_high.shape
    n = len(pieces)
    return pl.pallas_call(
        functools.partial(product_kernel, len(pieces[0])),
        out_shape=jax.ShapeDtypeStruct((n, rows, LANES), jnp.float32),
        in_specs=[pl.BlockSpec(memory_space=pltpu.VMEM)] * (2 + n * len(pieces[0])),
        out_specs=pl.BlockSpec(memory_space=pltpu.VMEM),
        scratch_shapes=[pltpu.VMEM((depth, 2 * LANES), jnp.bfloat16)] * 2,
        compiler_params=pltpu.CompilerParams(vmem_limit_bytes=12 * 2**20),
        cost_estimate=pl.CostEstimate(
            flops=6 * rows * depth * n * LANES,
            bytes_accessed=4 * depth * (rows + n * LANES),
            transcendentals=0,
        ),
        name="product",
    )(panel_high, panel_low, *[part for piece in pieces for part in piece])


def order_kernel(j_block, b_here, places_ref, *refs):
    *group_refs, out_ref, by_row = refs
    blocks = by_row.shape[0]
    slot = 0
    for ref in group_refs:
        for i in range(ref.shape[0]):
            by_row[places_ref[slot]] = ref[i].reshape(by_row.shape[1:])
            slot += 1
    for missing in range(slot, blocks):
        by_row[places_ref[missing]] = jnp.zeros(by_row.shape[1:], jnp.float32)
    rows, width = out_ref.shape
    virtual = blocks * b_here
    middle = j_block // 2
    lane = lax.broadcasted_iota(jnp.int32, (8, LANES), 1)
    moved = {}
    for tile in range(pl.cdiv(width, LANES)):
        first = tile * LANES
        last = min(first + LANES, width)
        value = None
        for j in range(j_block):
            turn = (j - middle) * (virtual - b_here) % LANES
            for block in range(blocks):
                start = j * virtual + block * b_here
                if start >= last or start + b_here <= first:
                    continue
                if (j, block) not in moved:
                    moved[j, block] = pltpu.roll(by_row[block], turn, 2) if turn else by_row[block]
                piece = moved[j, block]
                value = piece if value is None else jnp.where((lane >= start - first)[None], piece, value)
        out_ref[:, first:last] = value.reshape(rows, LANES)[:, : last - first]


def order(groups, places, j_block, b_here, row_block=80):
    blocks = places.shape[0]
    rows = groups[0].shape[1]
    width = blocks * b_here * j_block
    return pl.pallas_call(
        functools.partial(order_kernel, j_block, b_here),
        out_shape=jax.ShapeDtypeStruct((rows, width), jnp.float32),
        grid=(rows // row_block,),
        in_specs=[pl.BlockSpec(memory_space=pltpu.SMEM)]
        + [pl.BlockSpec((g.shape[0], row_block, LANES), lambda i: (0, i, 0)) for g in groups],
        out_specs=pl.BlockSpec((row_block, width), lambda i: (i, 0)),
        scratch_shapes=[pltpu.VMEM((blocks, row_block // 8, 8, LANES), jnp.float32)],
        compiler_params=pltpu.CompilerParams(vmem_limit_bytes=8 * 2**20),
        name="order",
    )(places, *groups)


def last_kernel(chunks, *refs):
    panel_high, panel_low, place_ref, *piece_refs, done_ref, out_ref, high, low = refs
    step = pl.program_id(0)

    @pl.when(step == 0)
    def _():
        fill([piece_refs[:chunks], piece_refs[chunks:]], high, low)

    rows = out_ref.shape[0]
    here = pl.ds(pl.multiple_of(step * rows, 16), rows)
    value = three_products(panel_high[here, :], panel_low[here, :], high[...], low[...])
    dot = functools.partial(jnp.dot, preferred_element_type=jnp.float32)
    first, second = split(value)
    out_ref[...] = done_ref[here, :] + (dot(first, place_ref[...]) + dot(second, place_ref[...]))


def last_product(panel_high, panel_low, pieces, place, done, row_block=400):
    rows, depth = panel_high.shape
    width = done.shape[1]
    whole = pl.BlockSpec(memory_space=pltpu.VMEM)
    return pl.pallas_call(
        functools.partial(last_kernel, len(pieces[0])),
        out_shape=jax.ShapeDtypeStruct((rows, width), jnp.float32),
        grid=(rows // row_block,),
        in_specs=[whole] * (4 + 2 * len(pieces[0])),
        out_specs=pl.BlockSpec((row_block, width), lambda i: (i, 0)),
        scratch_shapes=[pltpu.VMEM((depth, 2 * LANES), jnp.bfloat16)] * 2,
        compiler_params=pltpu.CompilerParams(vmem_limit_bytes=14 * 2**20),
        name="last",
    )(panel_high, panel_low, place, *[part for piece in pieces for part in piece], done)


def after(value, *others):
    return lax.optimization_barrier((value, *others))[0]


def per_device(integrals, amplitudes):
    rows_here = lax.axis_size("row")
    cols_here = lax.axis_size("col")
    k_here, occupied, b_here, virtual = amplitudes.shape
    j_block = occupied // cols_here
    k_total = k_here * cols_here
    row, col = lax.axis_index("row"), lax.axis_index("col")
    z, x, y, core = row // X, row % X, col // CORES, col % CORES

    q = jnp.arange(cols_here, dtype=jnp.int32)
    away = (q // CORES - y) % Y
    other = (q % CORES) ^ core
    virtual_blocks = rows_here * b_here
    turn = rotation(row, b_here, virtual_blocks, j_block)
    places = jnp.append(other * Y + away, turn).astype(jnp.int32)
    kept = regrid(amplitudes[0].transpose(1, 0, 2), places, j_block)
    kept, given = kept[:Y], kept[Y:]
    pairs = jnp.concatenate([kept, send_core(given)], axis=1)
    own = jnp.concatenate(
        [pairs[0], send_y(pairs[1], 1), send_y(pairs[3], -1), send_y(pairs[2], 2)], axis=0
    )
    panel = lax.all_gather(after(integrals.T, own), "col", axis=0, tiled=True)

    before, behind = send_first(own, 1), send_first(own, -1)
    half = own.shape[0] // 2
    across = jnp.concatenate([send_first(before[:half], 1), send_first(behind[half:], -1)], axis=0)
    line = [own, before, behind, across]
    line_offset = [0, -1, 1, 2]
    second_before = [send_second(piece, 1) for piece in line]
    second_after = [send_second(piece, -1) for piece in line]

    slot_of_away = jnp.array([0, 1, 3, 2], jnp.int32)
    k = jnp.arange(k_total, dtype=jnp.int32)
    slots = 2 * slot_of_away[(y - k // CORES) % Y] + ((k % CORES) ^ core)
    high, low = panels_by_k(after(panel, second_before[1], second_after[1]), slots, k_total)

    def place(i, second):
        first = line_offset[i]
        from_core0 = ((z + second) % Z) * X + (x + first) % X
        from_core1 = ((z + first) % Z) * X + (x + second) % X
        return jnp.where(core == 0, from_core0, from_core1)

    def both_sides(lines):
        return [(side[i],) for i in lines for side in (second_before, second_after)]

    products = [product(high, low, [(piece,) for piece in line])]
    places = [place(i, 0) for i in range(4)]
    second_across = [send_second(second_before[0], 1), send_second(second_after[1], -1)]
    products.append(product(high, low, both_sides((0, 1))))
    places += [place(i, second) for i in (0, 1) for second in (-1, 1)]
    second_across += [
        send_second(after(second_before[2], products[1]), 1),
        send_second(after(second_after[3], products[1]), -1),
    ]
    products.append(product(high, low, both_sides((2, 3))))
    places += [place(i, second) for i in (2, 3) for second in (-1, 1)]
    products.append(product(high, low, [(piece,) for piece in second_across[:2]]))
    places += [place(i, 2) for i in range(4)]
    places = jnp.stack(places).astype(jnp.int32)
    done = order(products, places, j_block, b_here)

    position = (jnp.arange(LANES, dtype=jnp.int32) - rotation(places[-2:, None], b_here, virtual_blocks, j_block)) % LANES
    column = (position // b_here) * virtual_blocks + places[-2:, None] * b_here + position % b_here
    column = jnp.where(position < j_block * b_here, column, -1).reshape(-1, 1)
    one_hot = (column == jnp.arange(done.shape[1], dtype=jnp.int32)).astype(jnp.bfloat16)
    return last_product(high, low, [(piece,) for piece in second_across[2:]], one_hot, done)


def solution(mesh):
    return jax.shard_map(
        per_device,
        mesh=mesh,
        in_specs=(P("row", "col"), P("col", None, "row", None)),
        out_specs=P("row", "col"),
        check_vma=False,
    )
```

```python
import functools

import jax
import jax.numpy as jnp
from jax import lax
from jax.experimental import pallas as pl
from jax.experimental.pallas import tpu as pltpu
from jax.sharding import PartitionSpec as P

Z, X, Y, CORES = 4, 4, 4, 2
AXES = ("row", "col")
LANES = 128


def permutation(move):
    pairs = []
    for z in range(Z):
        for x in range(X):
            for y in range(Y):
                for core in range(CORES):
                    to_z, to_x, to_y, to_core = move(z, x, y, core)
                    source = ((z * X + x) * Y + y) * CORES + core
                    target = (((to_z % Z) * X + to_x % X) * Y + to_y % Y) * CORES + to_core
                    pairs.append((source, target))
    return pairs


def send_y(value, distance):
    return lax.ppermute(value, AXES, permutation(lambda z, x, y, core: (z, x, y + distance, core)))


def send_core(value):
    return lax.ppermute(value, AXES, permutation(lambda z, x, y, core: (z, x, y, 1 - core)))


def send_first(value, distance):
    return lax.ppermute(
        value,
        AXES,
        permutation(lambda z, x, y, core: (z + distance * core, x + distance * (1 - core), y, core)),
    )


def send_second(value, distance):
    return lax.ppermute(
        value,
        AXES,
        permutation(lambda z, x, y, core: (z + distance * (1 - core), x + distance * core, y, core)),
    )


def rotation(block, b_here, virtual, j_block):
    middle = j_block // 2
    return (middle * (virtual - b_here) + block * b_here) % LANES


def regrid_kernel(j_block, place_ref, amp_ref, out_ref, rows):
    b_here, occupied, virtual = amp_ref.shape
    rows[...] = jnp.zeros_like(rows)
    for q in range(occupied // j_block):
        for j in range(j_block):
            rows[j * b_here : (j + 1) * b_here, :virtual] = amp_ref[:, q * j_block + j, :]
        out_ref[place_ref[q]] = pltpu.roll(rows[...].T[:virtual], place_ref[occupied // j_block], 1)


def regrid(amp, places, j_block):
    b_here, occupied, virtual = amp.shape
    blocks = occupied // j_block
    padded = pl.cdiv(virtual, LANES) * LANES
    return pl.pallas_call(
        functools.partial(regrid_kernel, j_block),
        out_shape=jax.ShapeDtypeStruct((blocks, virtual, LANES), jnp.float32),
        in_specs=[
            pl.BlockSpec(memory_space=pltpu.SMEM),
            pl.BlockSpec(memory_space=pltpu.VMEM),
        ],
        out_specs=pl.BlockSpec(memory_space=pltpu.VMEM),
        scratch_shapes=[pltpu.VMEM((LANES, padded), jnp.float32)],
        compiler_params=pltpu.CompilerParams(vmem_limit_bytes=8 * 2**20),
        name="regrid",
    )(places, amp)


def split(value):
    high = value.astype(jnp.bfloat16)
    low = (value - high.astype(jnp.float32)).astype(jnp.bfloat16)
    return high, low


def panel_kernel(k_total, slot_ref, *refs):
    *block_refs, high_ref, low_ref, joined, ordered = refs
    depth = joined.shape[0]
    virtual = depth // k_total
    part = 0
    for ref in block_refs:
        rows = ref.shape[0]
        joined[pl.ds(pl.multiple_of(slot_ref[k_total + part], 8), rows), :] = ref[...]
        part += 1
    for k in range(k_total):
        start = pl.multiple_of(slot_ref[k] * virtual, 8)
        ordered[pl.ds(start, virtual), :] = joined[pl.ds(k, virtual, stride=k_total), :]
    high_ref[...], low_ref[...] = split(ordered[...].T)


def panels_by_k(blocks, slots, k_total):
    depth = sum(block.shape[0] for block in blocks)
    rows = blocks[0].shape[1]
    return pl.pallas_call(
        functools.partial(panel_kernel, k_total),
        out_shape=[jax.ShapeDtypeStruct((rows, depth), jnp.bfloat16)] * 2,
        grid=(pl.cdiv(rows, LANES),),
        in_specs=[pl.BlockSpec(memory_space=pltpu.SMEM)]
        + [pl.BlockSpec((block.shape[0], LANES), lambda i: (0, i)) for block in blocks],
        out_specs=[pl.BlockSpec((LANES, depth), lambda i: (i, 0))] * 2,
        scratch_shapes=[pltpu.VMEM((depth, LANES), jnp.float32)] * 2,
        compiler_params=pltpu.CompilerParams(vmem_limit_bytes=14 * 2**20),
        name="panels",
    )(slots, *blocks)


def fill(near_ref, place_ref, first, piece_refs, high_ref, low_ref):
    near = near_ref.shape[1]
    for i, ref in enumerate(piece_refs):
        lanes = slice(i * LANES, (i + 1) * LANES)
        high_ref[:near, lanes], low_ref[:near, lanes] = split(near_ref[place_ref[first + i]])
        high_ref[near:, lanes], low_ref[near:, lanes] = split(ref[...])


def three_products(panel_high, panel_low, high, low):
    dot = functools.partial(jnp.dot, preferred_element_type=jnp.float32)
    return dot(panel_high, high) + (dot(panel_high, low) + dot(panel_low, high))


def product_kernel(place_ref, panel_high, panel_low, near_ref, *refs):
    *piece_refs, out_ref, high, low = refs
    for i in range(0, len(piece_refs), 2):
        fill(near_ref, place_ref, i, piece_refs[i : i + 2], high, low)
        value = three_products(panel_high[...], panel_low[...], high[...], low[...])
        out_ref[i] = value[:, :LANES]
        out_ref[i + 1] = value[:, LANES:]


def product(panel_high, panel_low, near, pieces, places):
    rows, depth = panel_high.shape
    n = len(pieces)
    return pl.pallas_call(
        product_kernel,
        out_shape=jax.ShapeDtypeStruct((n, rows, LANES), jnp.float32),
        in_specs=[pl.BlockSpec(memory_space=pltpu.SMEM)]
        + [pl.BlockSpec(memory_space=pltpu.VMEM)] * (3 + n),
        out_specs=pl.BlockSpec(memory_space=pltpu.VMEM),
        scratch_shapes=[pltpu.VMEM((depth, 2 * LANES), jnp.bfloat16)] * 2,
        compiler_params=pltpu.CompilerParams(vmem_limit_bytes=12 * 2**20),
        cost_estimate=pl.CostEstimate(
            flops=6 * rows * depth * n * LANES,
            bytes_accessed=4 * depth * (rows + n * LANES),
            transcendentals=0,
        ),
        name="product",
    )(jnp.stack(places).astype(jnp.int32), panel_high, panel_low, near, *pieces)


def order_kernel(j_block, b_here, places_ref, *refs):
    *group_refs, out_ref, by_row = refs
    blocks = by_row.shape[0]
    slot = 0
    for ref in group_refs:
        for i in range(ref.shape[0]):
            by_row[places_ref[slot]] = ref[i].reshape(by_row.shape[1:])
            slot += 1
    for missing in range(slot, blocks):
        by_row[places_ref[missing]] = jnp.zeros(by_row.shape[1:], jnp.float32)
    rows, width = out_ref.shape
    virtual = blocks * b_here
    middle = j_block // 2
    lane = lax.broadcasted_iota(jnp.int32, (8, LANES), 1)
    moved = {}
    for tile in range(pl.cdiv(width, LANES)):
        first = tile * LANES
        last = min(first + LANES, width)
        value = None
        for j in range(j_block):
            turn = (j - middle) * (virtual - b_here) % LANES
            for block in range(blocks):
                start = j * virtual + block * b_here
                if start >= last or start + b_here <= first:
                    continue
                if (j, block) not in moved:
                    moved[j, block] = pltpu.roll(by_row[block], turn, 2) if turn else by_row[block]
                piece = moved[j, block]
                value = piece if value is None else jnp.where((lane >= start - first)[None], piece, value)
        out_ref[:, first:last] = value.reshape(rows, LANES)[:, : last - first]


def order(groups, places, j_block, b_here, row_block=80):
    blocks = places.shape[0]
    rows = groups[0].shape[1]
    width = blocks * b_here * j_block
    return pl.pallas_call(
        functools.partial(order_kernel, j_block, b_here),
        out_shape=jax.ShapeDtypeStruct((rows, width), jnp.float32),
        grid=(rows // row_block,),
        in_specs=[pl.BlockSpec(memory_space=pltpu.SMEM)]
        + [pl.BlockSpec((g.shape[0], row_block, LANES), lambda i: (0, i, 0)) for g in groups],
        out_specs=pl.BlockSpec((row_block, width), lambda i: (i, 0)),
        scratch_shapes=[pltpu.VMEM((blocks, row_block // 8, 8, LANES), jnp.float32)],
        compiler_params=pltpu.CompilerParams(vmem_limit_bytes=8 * 2**20),
        name="order",
    )(places, *groups)


def last_kernel(places_ref, panel_high, panel_low, one_hot_ref, near_ref, *refs):
    *piece_refs, done_ref, out_ref, high, low = refs
    step = pl.program_id(0)

    @pl.when(step == 0)
    def _():
        fill(near_ref, places_ref, 0, piece_refs, high, low)

    rows = out_ref.shape[0]
    here = pl.ds(pl.multiple_of(step * rows, 16), rows)
    value = three_products(panel_high[here, :], panel_low[here, :], high[...], low[...])
    dot = functools.partial(jnp.dot, preferred_element_type=jnp.float32)
    first, second = split(value)
    out_ref[...] = done_ref[here, :] + (dot(first, one_hot_ref[...]) + dot(second, one_hot_ref[...]))


def last_product(panel_high, panel_low, near, pieces, places, one_hot, done, row_block=400):
    rows, depth = panel_high.shape
    width = done.shape[1]
    whole = pl.BlockSpec(memory_space=pltpu.VMEM)
    return pl.pallas_call(
        last_kernel,
        out_shape=jax.ShapeDtypeStruct((rows, width), jnp.float32),
        grid=(rows // row_block,),
        in_specs=[pl.BlockSpec(memory_space=pltpu.SMEM)] + [whole] * 7,
        out_specs=pl.BlockSpec((row_block, width), lambda i: (i, 0)),
        scratch_shapes=[pltpu.VMEM((depth, 2 * LANES), jnp.bfloat16)] * 2,
        compiler_params=pltpu.CompilerParams(vmem_limit_bytes=14 * 2**20),
        name="last",
    )(jnp.stack(places).astype(jnp.int32), panel_high, panel_low, one_hot, near, *pieces, done)


def after(value, *others):
    return lax.optimization_barrier((value, *others))[0]


def per_device(integrals, amplitudes):
    rows_here = lax.axis_size("row")
    cols_here = lax.axis_size("col")
    k_here, occupied, b_here, virtual = amplitudes.shape
    j_block = occupied // cols_here
    k_total = k_here * cols_here
    row, col = lax.axis_index("row"), lax.axis_index("col")
    z, x, y, core = row // X, row % X, col // CORES, col % CORES

    q = jnp.arange(cols_here, dtype=jnp.int32)
    away = (q // CORES - y) % Y
    other = (q % CORES) ^ core
    virtual_blocks = rows_here * b_here
    turn = rotation(row, b_here, virtual_blocks, j_block)
    places = jnp.append(other * Y + away, turn).astype(jnp.int32)
    kept = regrid(amplitudes[0].transpose(1, 0, 2), places, j_block)
    kept, given = kept[:Y], kept[Y:]
    pairs = jnp.concatenate([kept, send_core(given)], axis=1)
    near = lax.all_gather(pairs[0], "row", axis=0)
    own = jnp.concatenate(
        [send_y(pairs[1], 1), send_y(pairs[3], -1), send_y(pairs[2], 2)], axis=0
    )

    block = after(integrals.T, own)
    below, above = send_y(block, 1), send_y(block, -1)
    part = block.shape[0] // 2
    opposite = jnp.concatenate([send_y(below[:part], 1), send_y(above[part:], -1)], axis=0)
    blocks = [block, below, above, opposite]
    blocks += [send_core(each) for each in blocks]
    starts = [
        ((y + distance) % Y * CORES + side) * block.shape[0]
        for side in (core, 1 - core)
        for distance in (0, -1, 1, 2)
    ]

    before, behind = send_first(own, 1), send_first(own, -1)
    half = own.shape[0] // 2
    across = jnp.concatenate([send_first(before[:half], 1), send_first(behind[half:], -1)], axis=0)
    line = [own, before, behind, across]
    line_offset = [0, -1, 1, 2]
    second_before = [send_second(piece, 1) for piece in line]
    second_after = [send_second(piece, -1) for piece in line]

    slot_of_away = jnp.array([0, 1, 3, 2], jnp.int32)
    k = jnp.arange(k_total, dtype=jnp.int32)
    slots = 2 * slot_of_away[(y - k // CORES) % Y] + ((k % CORES) ^ core)
    slots = jnp.concatenate([slots, jnp.stack(starts)]).astype(jnp.int32)
    high, low = panels_by_k(blocks, slots, k_total)

    def place(i, second):
        first = line_offset[i]
        from_core0 = ((z + second) % Z) * X + (x + first) % X
        from_core1 = ((z + first) % Z) * X + (x + second) % X
        return jnp.where(core == 0, from_core0, from_core1)

    places = [[place(i, 0) for i in range(4)]]
    products = [product(high, low, near, line, places[0])]
    second_across = [send_second(second_before[0], 1), send_second(second_after[1], -1)]
    for lines in ((0, 1), (2, 3)):
        places.append([place(i, second) for i in lines for second in (-1, 1)])
        pieces = [side[i] for i in lines for side in (second_before, second_after)]
        products.append(product(high, low, near, pieces, places[-1]))
        if lines == (0, 1):
            second_across += [
                send_second(after(second_before[2], products[1]), 1),
                send_second(after(second_after[3], products[1]), -1),
            ]
    places.append([place(i, 2) for i in range(2)])
    products.append(product(high, low, near, second_across[:2], places[-1]))
    places.append([place(i, 2) for i in range(2, 4)])
    every = jnp.stack([p for group in places for p in group]).astype(jnp.int32)
    done = order(products, every, j_block, b_here)

    last = every[-2:, None]
    position = (jnp.arange(LANES, dtype=jnp.int32) - rotation(last, b_here, virtual_blocks, j_block)) % LANES
    column = (position // b_here) * virtual_blocks + last * b_here + position % b_here
    column = jnp.where(position < j_block * b_here, column, -1).reshape(-1, 1)
    one_hot = (column == jnp.arange(done.shape[1], dtype=jnp.int32)).astype(jnp.bfloat16)
    return last_product(high, low, near, second_across[2:], places[-1], one_hot, done)


def solution(mesh):
    return jax.shard_map(
        per_device,
        mesh=mesh,
        in_specs=(P("row", "col"), P("col", None, "row", None)),
        out_specs=P("row", "col"),
        check_vma=False,
    )
```

```python
import functools

import jax
import jax.numpy as jnp
from jax import lax
from jax.experimental import pallas as pl
from jax.experimental.pallas import tpu as pltpu
from jax.sharding import PartitionSpec as P

Z, X, Y, CORES = 4, 4, 4, 2
AXES = ("row", "col")
LANES = 128


def permutation(move):
    pairs = []
    for z in range(Z):
        for x in range(X):
            for y in range(Y):
                for core in range(CORES):
                    to_z, to_x, to_y, to_core = move(z, x, y, core)
                    source = ((z * X + x) * Y + y) * CORES + core
                    target = (((to_z % Z) * X + to_x % X) * Y + to_y % Y) * CORES + to_core
                    pairs.append((source, target))
    return pairs


def send_y(value, distance):
    return lax.ppermute(value, AXES, permutation(lambda z, x, y, core: (z, x, y + distance, core)))


def send_core(value):
    return lax.ppermute(value, AXES, permutation(lambda z, x, y, core: (z, x, y, 1 - core)))


def send_first(value, distance):
    return lax.ppermute(
        value,
        AXES,
        permutation(lambda z, x, y, core: (z + distance * core, x + distance * (1 - core), y, core)),
    )


def send_second(value, distance):
    return lax.ppermute(
        value,
        AXES,
        permutation(lambda z, x, y, core: (z + distance * (1 - core), x + distance * core, y, core)),
    )


def rotation(block, b_here, virtual, j_block):
    middle = j_block // 2
    return (middle * (virtual - b_here) + block * b_here) % LANES


def regrid_kernel(j_block, place_ref, amp_ref, out_ref, rows):
    b_here, occupied, virtual = amp_ref.shape
    rows[...] = jnp.zeros_like(rows)
    for q in range(occupied // j_block):
        for j in range(j_block):
            rows[j * b_here : (j + 1) * b_here, :virtual] = amp_ref[:, q * j_block + j, :]
        out_ref[place_ref[q]] = pltpu.roll(rows[...].T[:virtual], place_ref[occupied // j_block], 1)


def regrid(amp, places, j_block):
    b_here, occupied, virtual = amp.shape
    blocks = occupied // j_block
    padded = pl.cdiv(virtual, LANES) * LANES
    return pl.pallas_call(
        functools.partial(regrid_kernel, j_block),
        out_shape=jax.ShapeDtypeStruct((blocks, virtual, LANES), jnp.float32),
        in_specs=[
            pl.BlockSpec(memory_space=pltpu.SMEM),
            pl.BlockSpec(memory_space=pltpu.VMEM),
        ],
        out_specs=pl.BlockSpec(memory_space=pltpu.VMEM),
        scratch_shapes=[pltpu.VMEM((LANES, padded), jnp.float32)],
        compiler_params=pltpu.CompilerParams(vmem_limit_bytes=8 * 2**20),
        name="regrid",
    )(places, amp)


def split(value):
    high = value.astype(jnp.bfloat16)
    low = (value - high.astype(jnp.float32)).astype(jnp.bfloat16)
    return high, low


def panel_kernel(k_total, slot_ref, panel_ref, high_ref, low_ref, ordered):
    depth = panel_ref.shape[0]
    virtual = depth // k_total
    for k in range(k_total):
        start = pl.multiple_of(slot_ref[k] * virtual, 8)
        ordered[pl.ds(start, virtual), :] = panel_ref[pl.ds(k, virtual, stride=k_total), :]
    high_ref[...], low_ref[...] = split(ordered[...].T)


def panels_by_k(panel, slots, k_total):
    depth, rows = panel.shape
    return pl.pallas_call(
        functools.partial(panel_kernel, k_total),
        out_shape=[jax.ShapeDtypeStruct((rows, depth), jnp.bfloat16)] * 2,
        grid=(pl.cdiv(rows, LANES),),
        in_specs=[
            pl.BlockSpec(memory_space=pltpu.SMEM),
            pl.BlockSpec((depth, LANES), lambda i: (0, i)),
        ],
        out_specs=[pl.BlockSpec((LANES, depth), lambda i: (i, 0))] * 2,
        scratch_shapes=[pltpu.VMEM((depth, LANES), jnp.float32)],
        compiler_params=pltpu.CompilerParams(vmem_limit_bytes=34 * 2**20),
        cost_estimate=pl.CostEstimate(flops=12650000000, bytes_accessed=0, transcendentals=0),
        name="panels",
    )(slots, panel)


def fill(pieces, high_ref, low_ref):
    for i, parts in enumerate(pieces):
        start = 0
        for ref in parts:
            rows = slice(start, start + ref.shape[0])
            lanes = slice(i * LANES, (i + 1) * LANES)
            high_ref[rows, lanes], low_ref[rows, lanes] = split(ref[...])
            start += ref.shape[0]


def three_products(panel_high, panel_low, high, low):
    dot = functools.partial(jnp.dot, preferred_element_type=jnp.float32)
    return dot(panel_high, high) + (dot(panel_high, low) + dot(panel_low, high))


def product_kernel(chunks, *refs):
    panel_high, panel_low, *piece_refs, out_ref, high, low = refs
    pieces = [piece_refs[i : i + chunks] for i in range(0, len(piece_refs), chunks)]
    for i in range(0, len(pieces), 2):
        fill(pieces[i : i + 2], high, low)
        value = three_products(panel_high[...], panel_low[...], high[...], low[...])
        out_ref[i] = value[:, :LANES]
        out_ref[i + 1] = value[:, LANES:]


def product(panel_high, panel_low, pieces):
    rows, depth = panel_high.shape
    n = len(pieces)
    return pl.pallas_call(
        functools.partial(product_kernel, len(pieces[0])),
        out_shape=jax.ShapeDtypeStruct((n, rows, LANES), jnp.float32),
        in_specs=[pl.BlockSpec(memory_space=pltpu.VMEM)] * (2 + n * len(pieces[0])),
        out_specs=pl.BlockSpec(memory_space=pltpu.VMEM),
        scratch_shapes=[pltpu.VMEM((depth, 2 * LANES), jnp.bfloat16)] * 2,
        compiler_params=pltpu.CompilerParams(vmem_limit_bytes=12 * 2**20),
        cost_estimate=pl.CostEstimate(
            flops=6 * rows * depth * n * LANES,
            bytes_accessed=4 * depth * (rows + n * LANES),
            transcendentals=0,
        ),
        name="product",
    )(panel_high, panel_low, *[part for piece in pieces for part in piece])


def order_kernel(j_block, b_here, places_ref, *refs):
    *group_refs, out_ref, by_row = refs
    blocks = by_row.shape[0]
    slot = 0
    for ref in group_refs:
        for i in range(ref.shape[0]):
            by_row[places_ref[slot]] = ref[i].reshape(by_row.shape[1:])
            slot += 1
    for missing in range(slot, blocks):
        by_row[places_ref[missing]] = jnp.zeros(by_row.shape[1:], jnp.float32)
    rows, width = out_ref.shape
    virtual = blocks * b_here
    middle = j_block // 2
    lane = lax.broadcasted_iota(jnp.int32, (8, LANES), 1)
    moved = {}
    for tile in range(pl.cdiv(width, LANES)):
        first = tile * LANES
        last = min(first + LANES, width)
        value = None
        for j in range(j_block):
            turn = (j - middle) * (virtual - b_here) % LANES
            for block in range(blocks):
                start = j * virtual + block * b_here
                if start >= last or start + b_here <= first:
                    continue
                if (j, block) not in moved:
                    moved[j, block] = pltpu.roll(by_row[block], turn, 2) if turn else by_row[block]
                piece = moved[j, block]
                value = piece if value is None else jnp.where((lane >= start - first)[None], piece, value)
        out_ref[:, first:last] = value.reshape(rows, LANES)[:, : last - first]


def order(groups, places, j_block, b_here, row_block=80):
    blocks = places.shape[0]
    rows = groups[0].shape[1]
    width = blocks * b_here * j_block
    return pl.pallas_call(
        functools.partial(order_kernel, j_block, b_here),
        out_shape=jax.ShapeDtypeStruct((rows, width), jnp.float32),
        grid=(rows // row_block,),
        in_specs=[pl.BlockSpec(memory_space=pltpu.SMEM)]
        + [pl.BlockSpec((g.shape[0], row_block, LANES), lambda i: (0, i, 0)) for g in groups],
        out_specs=pl.BlockSpec((row_block, width), lambda i: (i, 0)),
        scratch_shapes=[pltpu.VMEM((blocks, row_block // 8, 8, LANES), jnp.float32)],
        compiler_params=pltpu.CompilerParams(vmem_limit_bytes=8 * 2**20),
        name="order",
    )(places, *groups)


def last_kernel(chunks, *refs):
    panel_high, panel_low, place_ref, *piece_refs, done_ref, out_ref, high, low = refs
    step = pl.program_id(0)

    @pl.when(step == 0)
    def _():
        fill([piece_refs[:chunks], piece_refs[chunks:]], high, low)

    rows = out_ref.shape[0]
    here = pl.ds(pl.multiple_of(step * rows, 16), rows)
    value = three_products(panel_high[here, :], panel_low[here, :], high[...], low[...])
    dot = functools.partial(jnp.dot, preferred_element_type=jnp.float32)
    first, second = split(value)
    out_ref[...] = done_ref[here, :] + (dot(first, place_ref[...]) + dot(second, place_ref[...]))


def last_product(panel_high, panel_low, pieces, place, done, row_block=400):
    rows, depth = panel_high.shape
    width = done.shape[1]
    whole = pl.BlockSpec(memory_space=pltpu.VMEM)
    return pl.pallas_call(
        functools.partial(last_kernel, len(pieces[0])),
        out_shape=jax.ShapeDtypeStruct((rows, width), jnp.float32),
        grid=(rows // row_block,),
        in_specs=[whole] * (4 + 2 * len(pieces[0])),
        out_specs=pl.BlockSpec((row_block, width), lambda i: (i, 0)),
        scratch_shapes=[pltpu.VMEM((depth, 2 * LANES), jnp.bfloat16)] * 2,
        compiler_params=pltpu.CompilerParams(vmem_limit_bytes=14 * 2**20),
        name="last",
    )(panel_high, panel_low, place, *[part for piece in pieces for part in piece], done)


def after(value, *others):
    return lax.optimization_barrier((value, *others))[0]


def per_device(integrals, amplitudes):
    rows_here = lax.axis_size("row")
    cols_here = lax.axis_size("col")
    k_here, occupied, b_here, virtual = amplitudes.shape
    j_block = occupied // cols_here
    k_total = k_here * cols_here
    row, col = lax.axis_index("row"), lax.axis_index("col")
    z, x, y, core = row // X, row % X, col // CORES, col % CORES

    q = jnp.arange(cols_here, dtype=jnp.int32)
    away = (q // CORES - y) % Y
    other = (q % CORES) ^ core
    virtual_blocks = rows_here * b_here
    turn = rotation(row, b_here, virtual_blocks, j_block)
    places = jnp.append(other * Y + away, turn).astype(jnp.int32)
    kept = regrid(amplitudes[0].transpose(1, 0, 2), places, j_block)
    kept, given = kept[:Y], kept[Y:]
    pairs = jnp.concatenate([kept, send_core(given)], axis=1)
    own = jnp.concatenate(
        [pairs[0], send_y(pairs[1], 1), send_y(pairs[3], -1), send_y(pairs[2], 2)], axis=0
    )
    panel = lax.all_gather(after(integrals.T, own), "col", axis=0, tiled=True)

    before, behind = send_first(own, 1), send_first(own, -1)
    half = own.shape[0] // 2
    across = jnp.concatenate([send_first(before[:half], 1), send_first(behind[half:], -1)], axis=0)
    line = [own, before, behind, across]
    line_offset = [0, -1, 1, 2]
    second_before = [send_second(piece, 1) for piece in line]
    second_after = [send_second(piece, -1) for piece in line]

    k = jnp.arange(k_total, dtype=jnp.int32)
    distance = (y - k // CORES) % Y
    slots = 2 * (distance ^ (distance >> 1)) + ((k % CORES) ^ core)
    high, low = panels_by_k(after(panel, across), slots, k_total)

    def place(i, second):
        first = line_offset[i]
        from_core0 = ((z + second) % Z) * X + (x + first) % X
        from_core1 = ((z + first) % Z) * X + (x + second) % X
        return jnp.where(core == 0, from_core0, from_core1)

    def both_sides(lines):
        return [(side[i],) for i in lines for side in (second_before, second_after)]

    products = [product(high, low, [(piece,) for piece in line])]
    places = [place(i, 0) for i in range(4)]
    second_across = [send_second(second_before[0], 1), send_second(second_after[1], -1)]
    products.append(product(high, low, both_sides((0, 1))))
    places += [place(i, second) for i in (0, 1) for second in (-1, 1)]
    second_across += [
        send_second(after(second_before[2], products[1]), 1),
        send_second(after(second_after[3], products[1]), -1),
    ]
    products.append(product(high, low, both_sides((2, 3))))
    places += [place(i, second) for i in (2, 3) for second in (-1, 1)]
    products.append(product(high, low, [(piece,) for piece in second_across[:2]]))
    places += [place(i, 2) for i in range(4)]
    places = jnp.stack(places).astype(jnp.int32)
    done = order(products, places, j_block, b_here)

    position = (jnp.arange(LANES, dtype=jnp.int32) - rotation(places[-2:, None], b_here, virtual_blocks, j_block)) % LANES
    column = (position // b_here) * virtual_blocks + places[-2:, None] * b_here + position % b_here
    column = jnp.where(position < j_block * b_here, column, -1).reshape(-1, 1)
    one_hot = (column == jnp.arange(done.shape[1], dtype=jnp.int32)).astype(jnp.bfloat16)
    return last_product(high, low, [(piece,) for piece in second_across[2:]], one_hot, done)


def solution(mesh):
    return jax.shard_map(
        per_device,
        mesh=mesh,
        in_specs=(P("row", "col"), P("col", None, "row", None)),
        out_specs=P("row", "col"),
        check_vma=False,
    )
```

```python
import functools

import jax
import jax.numpy as jnp
from jax import lax
from jax.experimental import pallas as pl
from jax.experimental.pallas import tpu as pltpu
from jax.sharding import PartitionSpec as P

Z, X, Y, CORES = 4, 4, 4, 2
AXES = ("row", "col")
LANES = 128


def permutation(move):
    pairs = []
    for z in range(Z):
        for x in range(X):
            for y in range(Y):
                for core in range(CORES):
                    to_z, to_x, to_y, to_core = move(z, x, y, core)
                    source = ((z * X + x) * Y + y) * CORES + core
                    target = (((to_z % Z) * X + to_x % X) * Y + to_y % Y) * CORES + to_core
                    pairs.append((source, target))
    return pairs


def send_y(value, distance):
    return lax.ppermute(value, AXES, permutation(lambda z, x, y, core: (z, x, y + distance, core)))


def send_core(value):
    return lax.ppermute(value, AXES, permutation(lambda z, x, y, core: (z, x, y, 1 - core)))


def send_first(value, distance):
    return lax.ppermute(
        value,
        AXES,
        permutation(lambda z, x, y, core: (z + distance * core, x + distance * (1 - core), y, core)),
    )


def send_second(value, distance):
    return lax.ppermute(
        value,
        AXES,
        permutation(lambda z, x, y, core: (z + distance * (1 - core), x + distance * core, y, core)),
    )


def rotation(block, b_here, virtual, j_block):
    middle = j_block // 2
    return (middle * (virtual - b_here) + block * b_here) % LANES


def regrid_kernel(j_block, place_ref, amp_ref, out_ref, rows):
    b_here, occupied, virtual = amp_ref.shape
    rows[...] = jnp.zeros_like(rows)
    for q in range(occupied // j_block):
        for j in range(j_block):
            rows[j * b_here : (j + 1) * b_here, :virtual] = amp_ref[:, q * j_block + j, :]
        out_ref[place_ref[q]] = pltpu.roll(rows[...].T[:virtual], place_ref[occupied // j_block], 1)


def regrid(amp, places, j_block):
    b_here, occupied, virtual = amp.shape
    blocks = occupied // j_block
    padded = pl.cdiv(virtual, LANES) * LANES
    return pl.pallas_call(
        functools.partial(regrid_kernel, j_block),
        out_shape=jax.ShapeDtypeStruct((blocks, virtual, LANES), jnp.float32),
        in_specs=[
            pl.BlockSpec(memory_space=pltpu.SMEM),
            pl.BlockSpec(memory_space=pltpu.VMEM),
        ],
        out_specs=pl.BlockSpec(memory_space=pltpu.VMEM),
        scratch_shapes=[pltpu.VMEM((LANES, padded), jnp.float32)],
        compiler_params=pltpu.CompilerParams(vmem_limit_bytes=8 * 2**20),
        name="regrid",
    )(places, amp)


def split(value):
    high = value.astype(jnp.bfloat16)
    low = (value - high.astype(jnp.float32)).astype(jnp.bfloat16)
    return high, low


def panel_kernel(k_total, slot_ref, panel_ref, high_ref, low_ref, ordered):
    depth = panel_ref.shape[0]
    virtual = depth // k_total
    for k in range(k_total):
        start = pl.multiple_of(slot_ref[k] * virtual, 8)
        ordered[pl.ds(start, virtual), :] = panel_ref[pl.ds(k, virtual, stride=k_total), :]
    high_ref[...], low_ref[...] = split(ordered[...].T)


def panels_by_k(panel, slots, k_total):
    depth, rows = panel.shape
    return pl.pallas_call(
        functools.partial(panel_kernel, k_total),
        out_shape=[jax.ShapeDtypeStruct((rows, depth), jnp.bfloat16)] * 2,
        grid=(pl.cdiv(rows, LANES),),
        in_specs=[
            pl.BlockSpec(memory_space=pltpu.SMEM),
            pl.BlockSpec((depth, LANES), lambda i: (0, i)),
        ],
        out_specs=[pl.BlockSpec((LANES, depth), lambda i: (i, 0))] * 2,
        scratch_shapes=[pltpu.VMEM((depth, LANES), jnp.float32)],
        compiler_params=pltpu.CompilerParams(vmem_limit_bytes=34 * 2**20),
        cost_estimate=pl.CostEstimate(flops=12650000000, bytes_accessed=0, transcendentals=0),
        name="panels",
    )(slots, panel)


def fill(pieces, high_ref, low_ref):
    for i, parts in enumerate(pieces):
        start = 0
        for ref in parts:
            rows = slice(start, start + ref.shape[0])
            lanes = slice(i * LANES, (i + 1) * LANES)
            high_ref[rows, lanes], low_ref[rows, lanes] = split(ref[...])
            start += ref.shape[0]


def three_products(panel_high, panel_low, high, low):
    dot = functools.partial(jnp.dot, preferred_element_type=jnp.float32)
    return dot(panel_high, high) + (dot(panel_high, low) + dot(panel_low, high))


def product_kernel(chunks, *refs):
    panel_high, panel_low, *piece_refs, out_ref, high, low = refs
    pieces = [piece_refs[i : i + chunks] for i in range(0, len(piece_refs), chunks)]
    for i in range(0, len(pieces), 2):
        fill(pieces[i : i + 2], high, low)
        value = three_products(panel_high[...], panel_low[...], high[...], low[...])
        out_ref[i] = value[:, :LANES]
        out_ref[i + 1] = value[:, LANES:]


def product(panel_high, panel_low, pieces):
    rows, depth = panel_high.shape
    n = len(pieces)
    return pl.pallas_call(
        functools.partial(product_kernel, len(pieces[0])),
        out_shape=jax.ShapeDtypeStruct((n, rows, LANES), jnp.float32),
        in_specs=[pl.BlockSpec(memory_space=pltpu.VMEM)] * (2 + n * len(pieces[0])),
        out_specs=pl.BlockSpec(memory_space=pltpu.VMEM),
        scratch_shapes=[pltpu.VMEM((depth, 2 * LANES), jnp.bfloat16)] * 2,
        compiler_params=pltpu.CompilerParams(vmem_limit_bytes=12 * 2**20),
        cost_estimate=pl.CostEstimate(
            flops=6 * rows * depth * n * LANES,
            bytes_accessed=4 * depth * (rows + n * LANES),
            transcendentals=0,
        ),
        name="product",
    )(panel_high, panel_low, *[part for piece in pieces for part in piece])


def order_kernel(j_block, b_here, places_ref, *refs):
    *group_refs, out_ref, by_row = refs
    blocks = by_row.shape[0]
    slot = 0
    for ref in group_refs:
        for i in range(ref.shape[0]):
            by_row[places_ref[slot]] = ref[i].reshape(by_row.shape[1:])
            slot += 1
    for missing in range(slot, blocks):
        by_row[places_ref[missing]] = jnp.zeros(by_row.shape[1:], jnp.float32)
    rows, width = out_ref.shape
    virtual = blocks * b_here
    middle = j_block // 2
    lane = lax.broadcasted_iota(jnp.int32, (8, LANES), 1)
    moved = {}
    for tile in range(pl.cdiv(width, LANES)):
        first = tile * LANES
        last = min(first + LANES, width)
        value = None
        for j in range(j_block):
            turn = (j - middle) * (virtual - b_here) % LANES
            for block in range(blocks):
                start = j * virtual + block * b_here
                if start >= last or start + b_here <= first:
                    continue
                if (j, block) not in moved:
                    moved[j, block] = pltpu.roll(by_row[block], turn, 2) if turn else by_row[block]
                piece = moved[j, block]
                value = piece if value is None else jnp.where((lane >= start - first)[None], piece, value)
        out_ref[:, first:last] = value.reshape(rows, LANES)[:, : last - first]


def order(groups, places, j_block, b_here, row_block=160):
    blocks = places.shape[0]
    rows = groups[0].shape[1]
    width = blocks * b_here * j_block
    return pl.pallas_call(
        functools.partial(order_kernel, j_block, b_here),
        out_shape=jax.ShapeDtypeStruct((rows, width), jnp.float32),
        grid=(rows // row_block,),
        in_specs=[pl.BlockSpec(memory_space=pltpu.SMEM)]
        + [pl.BlockSpec((g.shape[0], row_block, LANES), lambda i: (0, i, 0)) for g in groups],
        out_specs=pl.BlockSpec((row_block, width), lambda i: (i, 0)),
        scratch_shapes=[pltpu.VMEM((blocks, row_block // 8, 8, LANES), jnp.float32)],
        compiler_params=pltpu.CompilerParams(vmem_limit_bytes=12 * 2**20),
        name="order",
    )(places, *groups)


def last_kernel(chunks, *refs):
    panel_high, panel_low, place_ref, *piece_refs, done_ref, out_ref, high, low = refs
    step = pl.program_id(0)

    @pl.when(step == 0)
    def _():
        fill([piece_refs[:chunks], piece_refs[chunks:]], high, low)

    rows = out_ref.shape[0]
    here = pl.ds(pl.multiple_of(step * rows, 16), rows)
    value = three_products(panel_high[here, :], panel_low[here, :], high[...], low[...])
    dot = functools.partial(jnp.dot, preferred_element_type=jnp.float32)
    first, second = split(value)
    out_ref[...] = done_ref[here, :] + (dot(first, place_ref[...]) + dot(second, place_ref[...]))


def last_product(panel_high, panel_low, pieces, place, done, row_block=400):
    rows, depth = panel_high.shape
    width = done.shape[1]
    whole = pl.BlockSpec(memory_space=pltpu.VMEM)
    return pl.pallas_call(
        functools.partial(last_kernel, len(pieces[0])),
        out_shape=jax.ShapeDtypeStruct((rows, width), jnp.float32),
        grid=(rows // row_block,),
        in_specs=[whole] * (4 + 2 * len(pieces[0])),
        out_specs=pl.BlockSpec((row_block, width), lambda i: (i, 0)),
        scratch_shapes=[pltpu.VMEM((depth, 2 * LANES), jnp.bfloat16)] * 2,
        compiler_params=pltpu.CompilerParams(vmem_limit_bytes=14 * 2**20),
        name="last",
    )(panel_high, panel_low, place, *[part for piece in pieces for part in piece], done)


def after(value, *others):
    return lax.optimization_barrier((value, *others))[0]


def per_device(integrals, amplitudes):
    rows_here = lax.axis_size("row")
    cols_here = lax.axis_size("col")
    k_here, occupied, b_here, virtual = amplitudes.shape
    j_block = occupied // cols_here
    k_total = k_here * cols_here
    row, col = lax.axis_index("row"), lax.axis_index("col")
    z, x, y, core = row // X, row % X, col // CORES, col % CORES

    q = jnp.arange(cols_here, dtype=jnp.int32)
    away = (q // CORES - y) % Y
    other = (q % CORES) ^ core
    virtual_blocks = rows_here * b_here
    turn = rotation(row, b_here, virtual_blocks, j_block)
    places = jnp.append(other * Y + away, turn).astype(jnp.int32)
    kept = regrid(amplitudes[0].transpose(1, 0, 2), places, j_block)
    kept, given = kept[:Y], kept[Y:]
    pairs = jnp.concatenate([kept, send_core(given)], axis=1)
    own = jnp.concatenate(
        [pairs[0], send_y(pairs[1], 1), send_y(pairs[3], -1), send_y(pairs[2], 2)], axis=0
    )
    panel = lax.all_gather(after(integrals.T, own), "col", axis=0, tiled=True)

    before, behind = send_first(own, 1), send_first(own, -1)
    half = own.shape[0] // 2
    across = jnp.concatenate([send_first(before[:half], 1), send_first(behind[half:], -1)], axis=0)
    line = [own, before, behind, across]
    line_offset = [0, -1, 1, 2]
    second_before = [send_second(piece, 1) for piece in line]
    second_after = [send_second(piece, -1) for piece in line]

    k = jnp.arange(k_total, dtype=jnp.int32)
    distance = (y - k // CORES) % Y
    slots = 2 * (distance ^ (distance >> 1)) + ((k % CORES) ^ core)
    high, low = panels_by_k(after(panel, across), slots, k_total)

    def place(i, second):
        first = line_offset[i]
        from_core0 = ((z + second) % Z) * X + (x + first) % X
        from_core1 = ((z + first) % Z) * X + (x + second) % X
        return jnp.where(core == 0, from_core0, from_core1)

    def both_sides(lines):
        return [(side[i],) for i in lines for side in (second_before, second_after)]

    products = [product(high, low, [(piece,) for piece in line])]
    places = [place(i, 0) for i in range(4)]
    second_across = [send_second(second_before[0], 1), send_second(second_after[1], -1)]
    products.append(product(high, low, both_sides((0, 1))))
    places += [place(i, second) for i in (0, 1) for second in (-1, 1)]
    second_across += [
        send_second(after(second_before[2], products[1]), 1),
        send_second(after(second_after[3], products[1]), -1),
    ]
    products.append(product(high, low, both_sides((2, 3))))
    places += [place(i, second) for i in (2, 3) for second in (-1, 1)]
    products.append(product(high, low, [(piece,) for piece in second_across[:2]]))
    places += [place(i, 2) for i in range(4)]
    places = jnp.stack(places).astype(jnp.int32)
    done = order(products, places, j_block, b_here)

    position = (jnp.arange(LANES, dtype=jnp.int32) - rotation(places[-2:, None], b_here, virtual_blocks, j_block)) % LANES
    column = (position // b_here) * virtual_blocks + places[-2:, None] * b_here + position % b_here
    column = jnp.where(position < j_block * b_here, column, -1).reshape(-1, 1)
    one_hot = (column == jnp.arange(done.shape[1], dtype=jnp.int32)).astype(jnp.bfloat16)
    return last_product(high, low, [(piece,) for piece in second_across[2:]], one_hot, done)


def solution(mesh):
    return jax.shard_map(
        per_device,
        mesh=mesh,
        in_specs=(P("row", "col"), P("col", None, "row", None)),
        out_specs=P("row", "col"),
        check_vma=False,
    )
```

```python
import functools

import jax
import jax.numpy as jnp
from jax import lax
from jax.experimental import pallas as pl
from jax.experimental.pallas import tpu as pltpu
from jax.sharding import PartitionSpec as P

Z, X, Y, CORES = 4, 4, 4, 2
AXES = ("row", "col")
LANES = 128


def permutation(move):
    pairs = []
    for z in range(Z):
        for x in range(X):
            for y in range(Y):
                for core in range(CORES):
                    to_z, to_x, to_y, to_core = move(z, x, y, core)
                    source = ((z * X + x) * Y + y) * CORES + core
                    target = (((to_z % Z) * X + to_x % X) * Y + to_y % Y) * CORES + to_core
                    pairs.append((source, target))
    return pairs


def send_y(value, distance):
    return lax.ppermute(value, AXES, permutation(lambda z, x, y, core: (z, x, y + distance, core)))


def send_core(value):
    return lax.ppermute(value, AXES, permutation(lambda z, x, y, core: (z, x, y, 1 - core)))


def send_first(value, distance):
    return lax.ppermute(
        value,
        AXES,
        permutation(lambda z, x, y, core: (z + distance * core, x + distance * (1 - core), y, core)),
    )


def send_second(value, distance):
    return lax.ppermute(
        value,
        AXES,
        permutation(lambda z, x, y, core: (z + distance * (1 - core), x + distance * core, y, core)),
    )


def rotation(block, b_here, virtual, j_block):
    middle = j_block // 2
    return (middle * (virtual - b_here) + block * b_here) % LANES


def regrid_kernel(j_block, place_ref, amp_ref, out_ref, rows):
    b_here, occupied, virtual = amp_ref.shape
    rows[...] = jnp.zeros_like(rows)
    for q in range(occupied // j_block):
        for j in range(j_block):
            rows[j * b_here : (j + 1) * b_here, :virtual] = amp_ref[:, q * j_block + j, :]
        out_ref[place_ref[q]] = pltpu.roll(rows[...].T[:virtual], place_ref[occupied // j_block], 1)


def regrid(amp, places, j_block):
    b_here, occupied, virtual = amp.shape
    blocks = occupied // j_block
    padded = pl.cdiv(virtual, LANES) * LANES
    return pl.pallas_call(
        functools.partial(regrid_kernel, j_block),
        out_shape=jax.ShapeDtypeStruct((blocks, virtual, LANES), jnp.float32),
        in_specs=[
            pl.BlockSpec(memory_space=pltpu.SMEM),
            pl.BlockSpec(memory_space=pltpu.VMEM),
        ],
        out_specs=pl.BlockSpec(memory_space=pltpu.VMEM),
        scratch_shapes=[pltpu.VMEM((LANES, padded), jnp.float32)],
        compiler_params=pltpu.CompilerParams(vmem_limit_bytes=8 * 2**20),
        name="regrid",
    )(places, amp)


def split(value):
    high = value.astype(jnp.bfloat16)
    low = (value - high.astype(jnp.float32)).astype(jnp.bfloat16)
    return high, low


def panel_kernel(k_total, slot_ref, panel_ref, high_ref, low_ref, ordered):
    depth = panel_ref.shape[0]
    virtual = depth // k_total
    for k in range(k_total):
        start = pl.multiple_of(slot_ref[k] * virtual, 8)
        ordered[pl.ds(start, virtual), :] = panel_ref[pl.ds(k, virtual, stride=k_total), :]
    high_ref[...], low_ref[...] = split(ordered[...].T)


def panels_by_k(panel, slots, k_total):
    depth, rows = panel.shape
    return pl.pallas_call(
        functools.partial(panel_kernel, k_total),
        out_shape=[jax.ShapeDtypeStruct((rows, depth), jnp.bfloat16)] * 2,
        grid=(pl.cdiv(rows, LANES),),
        in_specs=[
            pl.BlockSpec(memory_space=pltpu.SMEM),
            pl.BlockSpec((depth, LANES), lambda i: (0, i)),
        ],
        out_specs=[pl.BlockSpec((LANES, depth), lambda i: (i, 0))] * 2,
        scratch_shapes=[pltpu.VMEM((depth, LANES), jnp.float32)],
        compiler_params=pltpu.CompilerParams(vmem_limit_bytes=34 * 2**20),
        cost_estimate=pl.CostEstimate(flops=12650000000, bytes_accessed=0, transcendentals=0),
        name="panels",
    )(slots, panel)


def fill(pieces, high_ref, low_ref):
    for i, parts in enumerate(pieces):
        start = 0
        for ref in parts:
            rows = slice(start, start + ref.shape[0])
            lanes = slice(i * LANES, (i + 1) * LANES)
            high_ref[rows, lanes], low_ref[rows, lanes] = split(ref[...])
            start += ref.shape[0]


def three_products(panel_high, panel_low, high, low):
    dot = functools.partial(jnp.dot, preferred_element_type=jnp.float32)
    return dot(panel_high, high) + (dot(panel_high, low) + dot(panel_low, high))


def product_kernel(chunks, *refs):
    panel_high, panel_low, *piece_refs, out_ref, high, low = refs
    pieces = [piece_refs[i : i + chunks] for i in range(0, len(piece_refs), chunks)]
    for i in range(0, len(pieces), 2):
        fill(pieces[i : i + 2], high, low)
        value = three_products(panel_high[...], panel_low[...], high[...], low[...])
        out_ref[i] = value[:, :LANES]
        out_ref[i + 1] = value[:, LANES:]


def product(panel_high, panel_low, pieces):
    rows, depth = panel_high.shape
    n = len(pieces)
    return pl.pallas_call(
        functools.partial(product_kernel, len(pieces[0])),
        out_shape=jax.ShapeDtypeStruct((n, rows, LANES), jnp.float32),
        in_specs=[pl.BlockSpec(memory_space=pltpu.VMEM)] * (2 + n * len(pieces[0])),
        out_specs=pl.BlockSpec(memory_space=pltpu.VMEM),
        scratch_shapes=[pltpu.VMEM((depth, 2 * LANES), jnp.bfloat16)] * 2,
        compiler_params=pltpu.CompilerParams(vmem_limit_bytes=12 * 2**20),
        cost_estimate=pl.CostEstimate(
            flops=6 * rows * depth * n * LANES,
            bytes_accessed=4 * depth * (rows + n * LANES),
            transcendentals=0,
        ),
        name="product",
    )(panel_high, panel_low, *[part for piece in pieces for part in piece])


def order_kernel(j_block, b_here, places_ref, *refs):
    *group_refs, out_ref, by_row = refs
    blocks = by_row.shape[0]
    slot = 0
    for ref in group_refs:
        for i in range(ref.shape[0]):
            by_row[places_ref[slot]] = ref[i].reshape(by_row.shape[1:])
            slot += 1
    for missing in range(slot, blocks):
        by_row[places_ref[missing]] = jnp.zeros(by_row.shape[1:], jnp.float32)
    rows, width = out_ref.shape
    virtual = blocks * b_here
    middle = j_block // 2
    lane = lax.broadcasted_iota(jnp.int32, (8, LANES), 1)
    moved = {}
    for tile in range(pl.cdiv(width, LANES)):
        first = tile * LANES
        last = min(first + LANES, width)
        value = None
        for j in range(j_block):
            turn = (j - middle) * (virtual - b_here) % LANES
            for block in range(blocks):
                start = j * virtual + block * b_here
                if start >= last or start + b_here <= first:
                    continue
                if (j, block) not in moved:
                    moved[j, block] = pltpu.roll(by_row[block], turn, 2) if turn else by_row[block]
                piece = moved[j, block]
                value = piece if value is None else jnp.where((lane >= start - first)[None], piece, value)
        out_ref[:, first:last] = value.reshape(rows, LANES)[:, : last - first]


def order(groups, places, j_block, b_here, row_block=400):
    blocks = places.shape[0]
    rows = groups[0].shape[1]
    width = blocks * b_here * j_block
    return pl.pallas_call(
        functools.partial(order_kernel, j_block, b_here),
        out_shape=jax.ShapeDtypeStruct((rows, width), jnp.float32),
        grid=(rows // row_block,),
        in_specs=[pl.BlockSpec(memory_space=pltpu.SMEM)]
        + [pl.BlockSpec((g.shape[0], row_block, LANES), lambda i: (0, i, 0)) for g in groups],
        out_specs=pl.BlockSpec((row_block, width), lambda i: (i, 0)),
        scratch_shapes=[pltpu.VMEM((blocks, row_block // 8, 8, LANES), jnp.float32)],
        compiler_params=pltpu.CompilerParams(vmem_limit_bytes=24 * 2**20),
        name="order",
    )(places, *groups)


def last_kernel(chunks, *refs):
    panel_high, panel_low, place_ref, *piece_refs, done_ref, out_ref, high, low = refs
    step = pl.program_id(0)

    @pl.when(step == 0)
    def _():
        fill([piece_refs[:chunks], piece_refs[chunks:]], high, low)

    rows = out_ref.shape[0]
    here = pl.ds(pl.multiple_of(step * rows, 16), rows)
    value = three_products(panel_high[here, :], panel_low[here, :], high[...], low[...])
    dot = functools.partial(jnp.dot, preferred_element_type=jnp.float32)
    first, second = split(value)
    out_ref[...] = done_ref[here, :] + (dot(first, place_ref[...]) + dot(second, place_ref[...]))


def last_product(panel_high, panel_low, pieces, place, done, row_block=400):
    rows, depth = panel_high.shape
    width = done.shape[1]
    whole = pl.BlockSpec(memory_space=pltpu.VMEM)
    return pl.pallas_call(
        functools.partial(last_kernel, len(pieces[0])),
        out_shape=jax.ShapeDtypeStruct((rows, width), jnp.float32),
        grid=(rows // row_block,),
        in_specs=[whole] * (4 + 2 * len(pieces[0])),
        out_specs=pl.BlockSpec((row_block, width), lambda i: (i, 0)),
        scratch_shapes=[pltpu.VMEM((depth, 2 * LANES), jnp.bfloat16)] * 2,
        compiler_params=pltpu.CompilerParams(vmem_limit_bytes=14 * 2**20),
        name="last",
    )(panel_high, panel_low, place, *[part for piece in pieces for part in piece], done)


def after(value, *others):
    return lax.optimization_barrier((value, *others))[0]


def per_device(integrals, amplitudes):
    rows_here = lax.axis_size("row")
    cols_here = lax.axis_size("col")
    k_here, occupied, b_here, virtual = amplitudes.shape
    j_block = occupied // cols_here
    k_total = k_here * cols_here
    row, col = lax.axis_index("row"), lax.axis_index("col")
    z, x, y, core = row // X, row % X, col // CORES, col % CORES

    q = jnp.arange(cols_here, dtype=jnp.int32)
    away = (q // CORES - y) % Y
    other = (q % CORES) ^ core
    virtual_blocks = rows_here * b_here
    turn = rotation(row, b_here, virtual_blocks, j_block)
    places = jnp.append(other * Y + away, turn).astype(jnp.int32)
    kept = regrid(amplitudes[0].transpose(1, 0, 2), places, j_block)
    kept, given = kept[:Y], kept[Y:]
    pairs = jnp.concatenate([kept, send_core(given)], axis=1)
    own = jnp.concatenate(
        [pairs[0], send_y(pairs[1], 1), send_y(pairs[3], -1), send_y(pairs[2], 2)], axis=0
    )
    panel = lax.all_gather(after(integrals.T, own), "col", axis=0, tiled=True)

    before, behind = send_first(own, 1), send_first(own, -1)
    half = own.shape[0] // 2
    across = jnp.concatenate([send_first(before[:half], 1), send_first(behind[half:], -1)], axis=0)
    line = [own, before, behind, across]
    line_offset = [0, -1, 1, 2]
    second_before = [send_second(piece, 1) for piece in line]
    second_after = [send_second(piece, -1) for piece in line]

    k = jnp.arange(k_total, dtype=jnp.int32)
    distance = (y - k // CORES) % Y
    slots = 2 * (distance ^ (distance >> 1)) + ((k % CORES) ^ core)
    high, low = panels_by_k(after(panel, across), slots, k_total)

    def place(i, second):
        first = line_offset[i]
        from_core0 = ((z + second) % Z) * X + (x + first) % X
        from_core1 = ((z + first) % Z) * X + (x + second) % X
        return jnp.where(core == 0, from_core0, from_core1)

    def both_sides(lines):
        return [(side[i],) for i in lines for side in (second_before, second_after)]

    products = [product(high, low, [(piece,) for piece in line])]
    places = [place(i, 0) for i in range(4)]
    second_across = [send_second(second_before[0], 1), send_second(second_after[1], -1)]
    products.append(product(high, low, both_sides((0, 1))))
    places += [place(i, second) for i in (0, 1) for second in (-1, 1)]
    second_across += [
        send_second(after(second_before[2], products[1]), 1),
        send_second(after(second_after[3], products[1]), -1),
    ]
    products.append(product(high, low, both_sides((2, 3))))
    places += [place(i, second) for i in (2, 3) for second in (-1, 1)]
    products.append(product(high, low, [(piece,) for piece in second_across[:2]]))
    places += [place(i, 2) for i in range(4)]
    places = jnp.stack(places).astype(jnp.int32)
    done = order(products, places, j_block, b_here)

    position = (jnp.arange(LANES, dtype=jnp.int32) - rotation(places[-2:, None], b_here, virtual_blocks, j_block)) % LANES
    column = (position // b_here) * virtual_blocks + places[-2:, None] * b_here + position % b_here
    column = jnp.where(position < j_block * b_here, column, -1).reshape(-1, 1)
    one_hot = (column == jnp.arange(done.shape[1], dtype=jnp.int32)).astype(jnp.bfloat16)
    return last_product(high, low, [(piece,) for piece in second_across[2:]], one_hot, done)


def solution(mesh):
    return jax.shard_map(
        per_device,
        mesh=mesh,
        in_specs=(P("row", "col"), P("col", None, "row", None)),
        out_specs=P("row", "col"),
        check_vma=False,
    )
```
